32 devices in a mesh: grp: 4 (over x, core), mem: 8 (over z, y).
Axes of the slice: x: 2, y: 2, z: 4, core: 2. Of those that a mesh axis runs over, the one named last changes fastest.
Arguments:
- vertex_table: float32 [32768, 128], P(('grp', 'mem')), may hold values from -1.8 to 1.8
- context_table: float32 [32768, 128], P(('grp', 'mem')), may hold values from -1.8 to 1.8
- edge_source: int32 [4, 4, 64, 512], P(None, 'grp', 'mem'), may hold values from 0 to 127
- edge_target: int32 [4, 4, 64, 512], P(None, 'grp', 'mem'), may hold values from 0 to 1534, as said below
- edge_weight: int32 [4, 4, 64, 512], P(None, 'grp', 'mem'), may hold values from 0 to 4, as said below
- negative_rows: int32 [4, 4, 64, 5, 512], P(None, 'grp', 'mem'), may hold values from 0 to 1535
Outputs:
- vertex_final: float32 [32768, 128], P(('grp', 'mem'))
- context_final: float32 [32768, 128], P(('grp', 'mem'))
The draws below stay inside these ranges and needn't reach their ends.
Inputs may be any that keep to these rules, and one draw needn't show every extreme that they name: For the slot's vertex row r = b * 128 + edge_source within its device (tile b of the device), edge_target - 256 - r lies in -256 to 255. `edge_weight`: in each tile the slots of nonzero weight come first; in every stratum each device has a tile whose 512 slots all have nonzero weight.
All inputs are finite; a program needn't handle non-finite values.
Results may differ from the reference program's by a relative error of at most 0.00014.
Values sent between devices are 32-bit elements; how exact they have to be, the bound alone decides.
A program may use at most 128 MiB of HBM per device.

```python
import jax
import jax.numpy as jnp

D = 128
R = 1024
STRIP = 256
ROWBLK = 128
SLOTS = 512
NEG = 5
GROUPS = 4
MEMBERS = 8
STRATA = 4
BLOCKS = 8
TILES = 64
N_MEM = 8


def edge_parts(key):
    keys = jax.random.split(jax.random.fold_in(key, 7), 5)
    shape = (STRATA, GROUPS, TILES, SLOTS)
    block_of_tile = jnp.arange(TILES, dtype=jnp.int32) % BLOCKS
    slot_number = jnp.arange(SLOTS, dtype=jnp.int32)[None, None, None, :]
    low_mark = (block_of_tile[None, None, :, None] == 0) & (slot_number == 0)
    high_mark = (block_of_tile[None, None, :, None] == BLOCKS - 1) & (slot_number == 0)
    source = jax.random.randint(keys[0], shape, 0, ROWBLK).astype(jnp.int32)
    source = jnp.where(low_mark, 0, jnp.where(high_mark, ROWBLK - 1, source)).astype(jnp.int32)
    block_start = block_of_tile * ROWBLK
    local_row = source + block_start[None, None, :, None]
    offset = jax.random.randint(keys[1], shape, -STRIP, STRIP).astype(jnp.int32)
    offset = jnp.where(low_mark, -STRIP, jnp.where(high_mark, STRIP - 1, offset)).astype(jnp.int32)
    target = local_row + STRIP + offset
    spread = jax.random.randint(keys[2], (STRATA, GROUPS, TILES, 1), 0, SLOTS).astype(jnp.int32)
    fill = SLOTS - spread * spread // SLOTS
    full_block = jax.random.randint(keys[3], (STRATA, GROUPS, N_MEM, 1, 1), 0, BLOCKS).astype(jnp.int32)
    block_number = jnp.arange(BLOCKS, dtype=jnp.int32)[None, None, None, :, None]
    fill = jnp.where(block_number == full_block, SLOTS, fill.reshape(STRATA, GROUPS, N_MEM, BLOCKS, 1))
    fill = fill.reshape(STRATA, GROUPS, TILES, 1)
    multiple = jax.random.randint(keys[4], shape, 1, 5).astype(jnp.int32)
    weight = jnp.where(slot_number < fill, multiple, 0).astype(jnp.int32)
    return (source, target, weight)


def draw_edge_source(key, part):
    return edge_parts(key)[0]


def draw_edge_target(key, part):
    return edge_parts(key)[1]


def draw_edge_weight(key, part):
    return edge_parts(key)[2]


def touch_ends(drawn, rng, smallest, high):
    place = [jax.random.randint(jax.random.fold_in(rng, axis), (), 0, length) for axis, length in enumerate(drawn.shape)]
    widest = drawn.shape.index(max(drawn.shape))
    neighbour = place[:widest] + [(place[widest] + 1) % drawn.shape[widest]] + place[widest + 1:]
    return drawn.at[tuple(place)].set(smallest).at[tuple(neighbour)].set(high)


def block_levels(stream_key, shape, pieces, least, high):
    level, own = 1.0, jax.random.fold_in(stream_key, 6)
    for dim, parts in pieces:
        draws = jnp.exp(jax.random.uniform(jax.random.fold_in(own, dim), (parts,), jnp.float32, least / len(pieces), high / len(pieces)))
        level = level * jnp.repeat(draws, shape[dim] // parts).reshape([-1 if axis == dim else 1 for axis in range(len(shape))])
    return level


def normal_values(rng, dims, deviation, most, cuts=(), kind=jnp.bfloat16):
    drawn = jax.random.normal(rng, dims, jnp.float32) * deviation
    if len(cuts) > 0:
        drawn = block_levels(rng, dims, cuts, -0.22, 0.18) * drawn
    return jnp.clip(drawn, min=-most, max=most).astype(kind)


def setup_inputs(seed: int = 0) -> dict:
    arg_keys = jax.random.split(jax.random.key(seed), 7)
    vertex_table = normal_values(arg_keys[0], (GROUPS * MEMBERS * R, D), 0.3, 1.8, ((0, 32),), jnp.float32)
    context_table = normal_values(arg_keys[1], (GROUPS * MEMBERS * R, D), 0.3, 1.8, ((0, 32),), jnp.float32)
    edge_source = draw_edge_source(jax.random.fold_in(arg_keys[6], 71), 0)
    edge_target = draw_edge_target(jax.random.fold_in(arg_keys[6], 71), 0)
    edge_weight = draw_edge_weight(jax.random.fold_in(arg_keys[6], 71), 0)
    negative_rows = touch_ends(jax.random.randint(arg_keys[5], (STRATA, GROUPS, TILES, NEG, SLOTS), 0, R + 2 * STRIP), jax.random.fold_in(arg_keys[5], 1), 0, (R + 2 * STRIP) - 1).astype(jnp.int32)
    return dict(vertex_table=vertex_table, context_table=context_table, edge_source=edge_source, edge_target=edge_target, edge_weight=edge_weight, negative_rows=negative_rows)


learning_rate = 0.05


def gray_code(value):
    return value ^ (value >> 1)


def reference(vertex_table, context_table, edge_source, edge_target, edge_weight, negative_rows):
    vertex = vertex_table.reshape(GROUPS, MEMBERS * R, D)
    context = context_table.reshape(GROUPS, MEMBERS * R, D)
    tile_index = jnp.arange(TILES, dtype=jnp.int32)
    row_base = (tile_index * ROWBLK)[:, None]
    slab_base = ((tile_index // BLOCKS) * R)[:, None]
    for stratum in range(STRATA):
        vertex_parts = []
        context_parts = [None] * GROUPS
        for group_index in range(GROUPS):
            partner = group_index ^ gray_code(stratum)
            padded = jnp.pad(context[partner], ((STRIP, STRIP), (0, 0)))
            vert_rows = row_base + edge_source[stratum, group_index]
            ctx_rows = slab_base + edge_target[stratum, group_index]
            noise_index = slab_base[:, :, None] + negative_rows[stratum, group_index]
            weight = edge_weight[stratum, group_index].astype(jnp.float32)
            picked = jnp.take(vertex[group_index], vert_rows, axis=0)
            target_vec = jnp.take(padded, ctx_rows, axis=0)
            noise_vec = jnp.take(padded, noise_index, axis=0)
            score = jnp.sum(picked * target_vec, axis=-1)
            noise_score = jnp.sum(picked[:, None] * noise_vec, axis=-1)
            positive_grad = (jax.nn.sigmoid(score) - 1.0) * weight
            negative_grad = jax.nn.sigmoid(noise_score) * weight[:, None]
            vert_delta = positive_grad[..., None] * target_vec + jnp.sum(negative_grad[..., None] * noise_vec, axis=1)
            vert_grad = jnp.zeros((MEMBERS * R, D), jnp.float32).at[vert_rows.reshape(-1)].add(vert_delta.reshape(-1, D))
            ctx_grad = jnp.zeros((MEMBERS * R + 2 * STRIP, D), jnp.float32)
            ctx_grad = ctx_grad.at[ctx_rows.reshape(-1)].add((positive_grad[..., None] * picked).reshape(-1, D))
            ctx_grad = ctx_grad.at[noise_index.reshape(-1)].add((negative_grad[..., None] * picked[:, None]).reshape(-1, D))
            vertex_parts.append(vertex[group_index] - learning_rate * vert_grad)
            context_parts[partner] = context[partner] - learning_rate * ctx_grad[STRIP:STRIP + MEMBERS * R]
        vertex = jnp.stack(vertex_parts)
        context = jnp.stack(context_parts)
    return vertex.reshape(GROUPS * MEMBERS * R, D), context.reshape(GROUPS * MEMBERS * R, D)
```

```python
import functools

import jax
import jax.numpy as jnp
from jax import lax
from jax.experimental import pallas as pl
from jax.experimental.pallas import tpu as pltpu
from jax.sharding import PartitionSpec as P

LR = 0.05
STRIP = 256
LANE = 256
BF = jnp.bfloat16
F8 = jnp.float8_e4m3fn
F32 = jnp.float32
NT = (((1,), (1,)), ((), ()))
NN = (((1,), (0,)), ((), ()))


def dot(a, b, dims=NN):
    return lax.dot_general(a, b, dims, preferred_element_type=F32)


def split(x):
    hi = x.astype(BF)
    return hi, (x - hi.astype(F32)).astype(BF)


def row_bf(x):
    return x.astype(F32).astype(BF)


def count_tile(b, src, tgt, w, neg, wneg, wpos, rowblk):
    slots = src.shape[1]
    chunks = wneg.shape[0]
    one = jnp.ones((), BF)
    zero = jnp.zeros((), BF)
    iota_r = row_bf(lax.broadcasted_iota(jnp.int32, (rowblk, slots), 0))
    iota_c = row_bf(lax.broadcasted_iota(jnp.int32, (LANE, slots), 0))
    s1 = jnp.where(iota_r == row_bf(src), row_bf(w), zero)

    def hot(x):
        return jnp.where(iota_c == row_bf(x & (LANE - 1)), one, zero).astype(F8)

    def tall(x, first, count):
        hi = (x >> 8) - first
        return jnp.concatenate(
            [(s1 * row_bf(jnp.where(hi == h, 1.0, 0.0))).astype(F8) for h in range(count)], axis=0
        )

    at = jnp.concatenate([tall(neg[n : n + 1], 0, chunks) for n in range(neg.shape[0])], axis=1)
    bt = jnp.concatenate([hot(neg[n : n + 1]) for n in range(neg.shape[0])], axis=1)
    cn = dot(at, bt, NT)
    first = b // 2
    cp = dot(tall(tgt, first, 3), hot(tgt), NT)
    rows = pl.ds(pl.multiple_of(b * rowblk, rowblk), rowblk)
    for h in range(chunks):
        wneg[h, rows, :] = cn[h * rowblk : (h + 1) * rowblk]
    for h in range(3):
        wpos[first + h, rows, :] = cp[h * rowblk : (h + 1) * rowblk]


def flip(g, value):
    bit = 1
    while bit <= value:
        if value & bit:
            g = g + bit - 2 * bit * ((g // bit) % 2)
        bit *= 2
    return g


def gray(t):
    return t ^ (t >> 1)


def remote(src, dst, send, recv, **where):
    return pltpu.make_async_remote_copy(
        src_ref=src, dst_ref=dst, send_sem=send, recv_sem=recv,
        device_id=where, device_id_type=pl.DeviceIdType.MESH,
    )


def kernel(
    v_in, c_in, e_src, e_tgt, e_w, e_neg, vout, cout,
    wneg, wpos, r_src, r_tgt, r_w, r_neg, vnew, vrecv, gs, gr, gm, gv, cext, chalo, vcat, vtcat,
    edge_send, edge_recv, halo_send, halo_recv, rim_send, rim_recv, v_send, v_recv,
):
    strata, blocks, slots = e_src.shape
    rows, width = v_in.shape
    rowblk = rows // blocks
    chunks = wneg.shape[1]
    zone = 2 * STRIP
    g = lax.axis_index("grp")
    m = lax.axis_index("mem")
    members = lax.axis_size("mem")
    groups = lax.axis_size("grp")
    has_down = m > 0
    has_up = m < members - 1

    barrier = pltpu.get_barrier_semaphore()
    for k in range(1, groups):
        pl.semaphore_signal(barrier, inc=1, device_id={"grp": flip(g, k)}, device_id_type=pl.DeviceIdType.MESH)

    @pl.when(has_down)
    def _():
        pl.semaphore_signal(barrier, inc=1, device_id={"mem": m - 1}, device_id_type=pl.DeviceIdType.MESH)

    @pl.when(has_up)
    def _():
        pl.semaphore_signal(barrier, inc=1, device_id={"mem": m + 1}, device_id_type=pl.DeviceIdType.MESH)

    pl.semaphore_wait(barrier, groups - 1 + jnp.where(has_down, 1, 0) + jnp.where(has_up, 1, 0))

    def halo(side):
        if side == 0:
            return remote(c_in.at[0:STRIP], chalo.at[1], halo_send.at[0], halo_recv.at[1], mem=m - 1)
        return remote(c_in.at[rows - STRIP : rows], chalo.at[0], halo_send.at[1], halo_recv.at[0], mem=m + 1)

    def rim(t, side):
        last = t == strata - 1
        if side == 0:
            span = slice(0, STRIP if last else zone)
            return remote(gs.at[t, 0, span], gr.at[t, 1, span], rim_send.at[t, 0], rim_recv.at[t, 1], mem=m - 1)
        span = slice(STRIP if last else 0, zone)
        return remote(gs.at[t, 1, span], gr.at[t, 0, span], rim_send.at[t, 1], rim_recv.at[t, 0], mem=m + 1)

    def hop(t, part):
        step = gray(t) ^ gray((t + 1) % strata)
        span = slice(part * rows // 2, (part + 1) * rows // 2)
        return remote(
            vnew.at[t, span], vrecv.at[t, span], v_send.at[t, part], v_recv.at[t, part], grp=flip(g, step)
        )

    def edge(t, k):
        a = (e_src, e_tgt, e_w, e_neg)[k]
        z = (r_src, r_tgt, r_w, r_neg)[k]
        i = (t - 1) * 4 + k
        return remote(a.at[t], z.at[t - 1], edge_send.at[i], edge_recv.at[i], grp=flip(g, gray(t)))

    def both(action):
        @pl.when(has_down)
        def _():
            action(0)

        @pl.when(has_up)
        def _():
            action(1)

    both(lambda side: halo(side).start())
    for t in range(1, strata):
        for k in range(4):
            edge(t, k).start()

    def counts(t):
        if t == 0:
            a, b_, c, d = e_src.at[0], e_tgt.at[0], e_w.at[0], e_neg.at[0]
        else:
            for k in range(4):
                edge(t, k).wait_recv()
            a, b_, c, d = r_src.at[t - 1], r_tgt.at[t - 1], r_w.at[t - 1], r_neg.at[t - 1]

        @pl.loop(0, blocks, unroll=2)
        def _(b):
            one = pl.ds(b, 1)
            count_tile(b, a[one, :], b_[one, :], c[one, :], jnp.concatenate([d[n, one, :] for n in range(d.shape[0])], axis=0), wneg.at[t % 2], wpos.at[t % 2], rowblk)

    for slot in range(2):
        for h in range(chunks):
            wpos[slot, h] = jnp.zeros((rows, LANE), F32)
    counts(0)

    cext[STRIP : STRIP + rows] = c_in[...]
    for side in range(2):
        there = has_down if side == 0 else has_up
        span = slice(0, STRIP) if side == 0 else slice(STRIP + rows, rows + 2 * STRIP)

        @pl.when(there)
        def _():
            halo(1 - side).wait_recv()
            cext[span] = chalo[side]

        @pl.when(jnp.logical_not(there))
        def _():
            cext[span] = jnp.zeros((STRIP, width), F32)

    def chunk(slot, h, r0, nrows):
        part = slice(r0, r0 + nrows)
        c = cext[pl.ds(pl.multiple_of(h * LANE, LANE), LANE), :]
        chi, clo = split(c)
        cc = jnp.concatenate([chi, chi], axis=1)
        ccat = jnp.concatenate([chi, clo], axis=1)
        score = dot(vcat[part], cc, NT) + dot(vcat[part, :width], clo, NT)
        sig = 0.5 * jnp.tanh(0.5 * score) + 0.5
        pos = wpos[slot, h, part, :]
        gg = wneg[slot, h, part, :] * sig + pos * (sig - 1.0)
        g1, g2 = split(gg)
        wide = dot(g1, ccat)
        gv[part] += wide[:, :width] + wide[:, width:] + dot(g2, chi)
        tall = dot(vtcat[:, part], g1)
        gt = tall[:width] + tall[width:] + dot(vtcat[:width, part], g2)
        return gt.T

    for t in range(strata):
        slot = t % 2
        if t == 0:
            v_now = v_in
        else:
            for part in range(2):
                hop(t - 1, part).wait_recv()
            v_now = vrecv.at[t - 1]
        v = v_now[...]
        vhi, vlo = split(v)
        vcat[...] = jnp.concatenate([vhi, vlo], axis=1)
        vcat_t = split(v.T)
        vtcat[...] = jnp.concatenate(vcat_t, axis=0)
        gv[...] = jnp.zeros((rows, width), F32)
        far = gray(t) ^ gray((t + 1) % strata) > 1
        parts = 2 if far else 1
        nrows = rows // parts
        for part in range(parts):
            r0 = part * nrows

            @pl.loop(0, 4, unroll=2)
            def _(j):
                side = j // 2
                span = pl.ds(pl.multiple_of((j % 2) * LANE, LANE), LANE)
                gt = chunk(slot, j + 2 * side, r0, nrows)
                if part == 0:
                    gs[t, side, span, :] = gt
                else:
                    gs[t, side, span, :] += gt

            if part == parts - 1:
                both(lambda side: rim(t, side).start())

            @pl.loop(0, 2, unroll=2)
            def _(j):
                span = pl.ds(pl.multiple_of(j * LANE, LANE), LANE)
                gt = chunk(slot, j + 2, r0, nrows)
                if part == 0:
                    gm[span, :] = gt
                else:
                    gm[span, :] += gt

            mine = slice(r0, r0 + nrows)
            vnew[t, mine] = v_now[mine] - LR * gv[mine]
            for half in range(2) if parts == 1 else (part,):
                hop(t, half).start()
        if t < strata - 1:
            cext[zone : zone + rows - zone] -= LR * gm[...]
            counts(t + 1)
            for side in range(2):
                there = has_down if side == 0 else has_up
                base = 0 if side == 0 else rows
                own = slice(base + STRIP, base + zone) if side == 0 else slice(base, base + STRIP)
                off = slice(STRIP, zone) if side == 0 else slice(0, STRIP)

                @pl.when(there)
                def _():
                    rim(t, 1 - side).wait_recv()
                    cext[base : base + zone] -= LR * (gs[t, side] + gr[t, side])

                @pl.when(jnp.logical_not(there))
                def _():
                    cext[own] -= LR * gs[t, side, off]
        else:
            cout[STRIP : rows - STRIP] = cext[zone:rows] - LR * gm[...]
            for side in range(2):
                there = has_down if side == 0 else has_up
                base = 0 if side == 0 else rows
                own = slice(base + STRIP, base + zone) if side == 0 else slice(base, base + STRIP)
                off = slice(STRIP, zone) if side == 0 else slice(0, STRIP)
                to = slice(0, STRIP) if side == 0 else slice(rows - STRIP, rows)

                @pl.when(there)
                def _():
                    rim(t, 1 - side).wait_recv()
                    cout[to] = cext[own] - LR * (gs[t, side, off] + gr[t, side, off])

                @pl.when(jnp.logical_not(there))
                def _():
                    cout[to] = cext[own] - LR * gs[t, side, off]

            for part in range(2):
                hop(t, part).wait_recv()
            vout[...] = vrecv[t]

    both(lambda side: halo(side).wait_send())
    for t in range(strata):
        both(lambda side: rim(t, side).wait_send())
        for part in range(2):
            hop(t, part).wait_send()
        if t:
            for k in range(4):
                edge(t, k).wait_send()


def hand_on(v, c, vout, cout):
    vout[...] = v[...]
    cout[...] = c[...]


def local(vertex, context, edge_source, edge_target, edge_weight, negative_rows):
    strata, _, blocks, slots = edge_source.shape
    negs = negative_rows.shape[3]
    rows, width = vertex.shape
    ext = rows + 2 * STRIP
    chunks = ext // LANE
    flat = (strata, blocks, slots)
    vm = pl.BlockSpec(memory_space=pltpu.VMEM)
    sem = pltpu.SemaphoreType.DMA
    i32 = jnp.int32
    final = pl.pallas_call(
        kernel,
        out_shape=(jax.ShapeDtypeStruct((rows, width), F32),) * 2,
        in_specs=[vm] * 6,
        out_specs=(vm, vm),
        scratch_shapes=[
            pltpu.VMEM((2, chunks, rows, LANE), F32),
            pltpu.VMEM((2, chunks, rows, LANE), F32),
            pltpu.VMEM((strata - 1, blocks, slots), i32),
            pltpu.VMEM((strata - 1, blocks, slots), i32),
            pltpu.VMEM((strata - 1, blocks, slots), i32),
            pltpu.VMEM((strata - 1, negs, blocks, slots), i32),
            pltpu.VMEM((strata, rows, width), F32),
            pltpu.VMEM((strata, rows, width), F32),
            pltpu.VMEM((strata, 2, 2 * STRIP, width), F32),
            pltpu.VMEM((strata, 2, 2 * STRIP, width), F32),
            pltpu.VMEM((rows - 2 * STRIP, width), F32),
            pltpu.VMEM((rows, width), F32),
            pltpu.VMEM((ext, width), F32),
            pltpu.VMEM((2, STRIP, width), F32),
            pltpu.VMEM((rows, 2 * width), BF),
            pltpu.VMEM((2 * width, rows), BF),
            sem((4 * (strata - 1),)),
            sem((4 * (strata - 1),)),
            sem((2,)),
            sem((2,)),
            sem((strata, 2)),
            sem((strata, 2)),
            sem((strata, 2)),
            sem((strata, 2)),
        ],
        compiler_params=pltpu.CompilerParams(
            collective_id=0, has_side_effects=True, vmem_limit_bytes=60 * 1024 * 1024
        ),
    )(
        vertex,
        context,
        edge_source.reshape(flat),
        edge_target.reshape(flat),
        edge_weight.reshape(flat),
        negative_rows.reshape(strata, blocks, negs, slots).transpose(0, 2, 1, 3),
    )
    return pl.pallas_call(
        hand_on,
        out_shape=(jax.ShapeDtypeStruct((rows, width), F32),) * 2,
        in_specs=[vm] * 2,
        out_specs=(vm, vm),
    )(*final)


def solution(mesh):
    lead = P(("grp", "mem"), None)
    edges = P(None, "grp", "mem", None)
    return jax.shard_map(
        local,
        mesh=mesh,
        in_specs=(lead, lead, edges, edges, edges, P(None, "grp", "mem", None, None)),
        out_specs=(lead, lead),
        check_vma=False,
    )
```

```python
import functools

import jax
import jax.numpy as jnp
from jax import lax
from jax.experimental import pallas as pl
from jax.experimental.pallas import tpu as pltpu
from jax.sharding import PartitionSpec as P

LR = 0.05
STRIP = 256
LANE = 256
BF = jnp.bfloat16
F8 = jnp.float8_e4m3fn
F32 = jnp.float32
NT = (((1,), (1,)), ((), ()))
NN = (((1,), (0,)), ((), ()))
TN = (((0,), (0,)), ((), ()))
UP = 256.0
TOP = 448.0


def dot(a, b, dims=NN):
    return lax.dot_general(a, b, dims, preferred_element_type=F32)


def split(x):
    hi = x.astype(BF)
    return hi, (x - hi.astype(F32)).astype(BF)


def small(x, scale):
    return jnp.clip(x.astype(F32) * scale, -TOP, TOP).astype(F8)


def row_bf(x):
    return x.astype(F32).astype(BF)


def count_tile(b, src, tgt, w, neg, wsum, wdif, rowblk):
    slots = src.shape[1]
    chunks = wsum.shape[0]
    one = jnp.ones((), BF)
    zero = jnp.zeros((), BF)
    iota_r = row_bf(lax.broadcasted_iota(jnp.int32, (rowblk, slots), 0))
    iota_c = row_bf(lax.broadcasted_iota(jnp.int32, (LANE, slots), 0))
    s1 = jnp.where(iota_r == row_bf(src), row_bf(w) * jnp.asarray(0.5, BF), zero)

    def hot(x):
        return jnp.where(iota_c == row_bf(x & (LANE - 1)), one, zero).astype(F8)

    def tall(x, first, count):
        hi = (x >> 8) - first
        return jnp.concatenate(
            [(s1 * row_bf(jnp.where(hi == h, 1.0, 0.0))).astype(F8) for h in range(count)], axis=0
        )

    at = jnp.concatenate([tall(neg[n : n + 1], 0, chunks) for n in range(neg.shape[0])], axis=1)
    bt = jnp.concatenate([hot(neg[n : n + 1]) for n in range(neg.shape[0])], axis=1)
    cn = dot(at, bt, NT)
    first = b // 2
    cp = dot(tall(tgt, first, 3), hot(tgt), NT)
    rows = pl.ds(pl.multiple_of(b * rowblk, rowblk), rowblk)
    for h in range(chunks):
        wsum[h, rows, :] = cn[h * rowblk : (h + 1) * rowblk]
        wdif[h, rows, :] = cn[h * rowblk : (h + 1) * rowblk]
    for h in range(3):
        wsum[first + h, rows, :] += cp[h * rowblk : (h + 1) * rowblk]
        wdif[first + h, rows, :] -= cp[h * rowblk : (h + 1) * rowblk]


def flip(g, value):
    bit = 1
    while bit <= value:
        if value & bit:
            g = g + bit - 2 * bit * ((g // bit) % 2)
        bit *= 2
    return g


def gray(t):
    return t ^ (t >> 1)


def remote(src, dst, send, recv, **where):
    return pltpu.make_async_remote_copy(
        src_ref=src, dst_ref=dst, send_sem=send, recv_sem=recv,
        device_id=where, device_id_type=pl.DeviceIdType.MESH,
    )


def kernel(
    v_in, c_in, e_src, e_tgt, e_w, e_neg, vout, cout,
    wsum, wdif, r_src, r_tgt, r_w, r_neg, vnew, vrecv, gs, gr, gm, gv, cext, cnext, clast, cfin, chalo, vcat, v8,
    edge_send, edge_recv, halo_send, halo_recv, rim_send, rim_recv, v_send, v_recv, c_send, c_recv,
):
    strata, blocks, slots = e_src.shape
    rows, width = v_in.shape
    rowblk = rows // blocks
    chunks = wsum.shape[1]
    zone = 2 * STRIP
    g = lax.axis_index("grp")
    m = lax.axis_index("mem")
    members = lax.axis_size("mem")
    has_down = m > 0
    has_up = m < members - 1
    near, far = flip(g, 1), flip(g, 2)

    barrier = pltpu.get_barrier_semaphore()
    for partner in (near, far):
        pl.semaphore_signal(barrier, inc=1, device_id={"grp": partner}, device_id_type=pl.DeviceIdType.MESH)

    @pl.when(has_down)
    def _():
        pl.semaphore_signal(barrier, inc=1, device_id={"mem": m - 1}, device_id_type=pl.DeviceIdType.MESH)

    @pl.when(has_up)
    def _():
        pl.semaphore_signal(barrier, inc=1, device_id={"mem": m + 1}, device_id_type=pl.DeviceIdType.MESH)

    pl.semaphore_wait(barrier, 2 + jnp.where(has_down, 1, 0) + jnp.where(has_up, 1, 0))

    def halo(side):
        if side == 0:
            return remote(c_in.at[0:STRIP], chalo.at[1], halo_send.at[0], halo_recv.at[1], mem=m - 1)
        return remote(c_in.at[rows - STRIP : rows], chalo.at[0], halo_send.at[1], halo_recv.at[0], mem=m + 1)

    def rim(t, side):
        last = t == strata - 1
        if side == 0:
            span = slice(0, STRIP if last else zone)
            return remote(gs.at[t, 0, span], gr.at[t, 1, span], rim_send.at[t, 0], rim_recv.at[t, 1], mem=m - 1)
        span = slice(STRIP if last else 0, zone)
        return remote(gs.at[t, 1, span], gr.at[t, 0, span], rim_send.at[t, 1], rim_recv.at[t, 0], mem=m + 1)

    def hop(t):
        i = t // 2
        return remote(vnew.at[i], vrecv.at[i], v_send.at[i], v_recv.at[i], grp=near)

    def area(side):
        return slice(zone, rows) if side == 2 else slice(side * rows, side * rows + zone)

    def own(side):
        return (slice(0, STRIP), slice(rows - STRIP, rows), slice(STRIP, rows - STRIP))[side]

    def cross(side):
        span = area(side)
        return remote(cext.at[span], cnext.at[span], c_send.at[0, side], c_recv.at[0, side], grp=far)

    def home(side):
        span = own(side)
        return remote(clast.at[span], cfin.at[span], c_send.at[1, side], c_recv.at[1, side], grp=far)

    def edge(t, k):
        a = (e_src, e_tgt, e_w, e_neg)[k]
        z = (r_src, r_tgt, r_w, r_neg)[k]
        i = (t - 1) * 4 + k
        return remote(a.at[t], z.at[t - 1], edge_send.at[i], edge_recv.at[i], grp=near)

    def guard(side, action):
        @pl.when(has_down if side == 0 else has_up)
        def _():
            action()

    def counts(t, between=None):
        if t in (0, strata - 1):
            a, b_, c, d = e_src.at[t], e_tgt.at[t], e_w.at[t], e_neg.at[t]
        else:
            for k in range(4):
                edge(t, k).wait_recv()
            a, b_, c, d = r_src.at[t - 1], r_tgt.at[t - 1], r_w.at[t - 1], r_neg.at[t - 1]

        def run(lo, hi):
            @pl.loop(lo, hi, unroll=2)
            def _(b):
                one = pl.ds(b, 1)
                count_tile(b, a[one, :], b_[one, :], c[one, :], jnp.concatenate([d[n, one, :] for n in range(d.shape[0])], axis=0), wsum.at[t % 2], wdif.at[t % 2], rowblk)

        if between is None:
            run(0, blocks)
        else:
            run(0, blocks // 2)
            between()
            run(blocks // 2, blocks)

    def enter(side):
        there = has_down if side == 0 else has_up
        span = slice(0, STRIP) if side == 0 else slice(STRIP + rows, rows + 2 * STRIP)

        @pl.when(there)
        def _():
            halo(1 - side).wait_recv()
            cext[span] = chalo[side]

        @pl.when(jnp.logical_not(there))
        def _():
            cext[span] = jnp.zeros((STRIP, width), F32)

    def settle(t, side, ctx):
        there = has_down if side == 0 else has_up
        base = side * rows
        mine = slice(base + STRIP, base + zone) if side == 0 else slice(base, base + STRIP)
        off = slice(STRIP, zone) if side == 0 else slice(0, STRIP)

        @pl.when(there)
        def _():
            rim(t, 1 - side).wait_recv()
            ctx[base : base + zone] -= LR * (gs[t, side] + gr[t, side])

        @pl.when(jnp.logical_not(there))
        def _():
            ctx[mine] -= LR * gs[t, side, off]

    def finish(side):
        t = strata - 1
        there = has_down if side == 0 else has_up
        base = side * rows
        mine = slice(base + STRIP, base + zone) if side == 0 else slice(base, base + STRIP)
        off = slice(STRIP, zone) if side == 0 else slice(0, STRIP)
        to = own(side)

        @pl.when(there)
        def _():
            rim(t, 1 - side).wait_recv()
            clast[to] = cnext[mine] - LR * (gs[t, side, off] + gr[t, side, off])

        @pl.when(jnp.logical_not(there))
        def _():
            clast[to] = cnext[mine] - LR * gs[t, side, off]

        home(side).start()

    def chunk(slot, ctx, h):
        c = ctx[pl.ds(pl.multiple_of(h * LANE, LANE), LANE), :]
        chi, clo = split(c)
        ccat = jnp.concatenate([chi, clo], axis=1)
        chalf = (chi.astype(F32) * 0.5).astype(BF)
        c8 = jnp.concatenate([small(chi, 0.5), small(clo, 0.5 * UP)], axis=1)
        half = dot(vcat[:, :width], chalf, NT) + dot(v8[...], c8, NT) * (1.0 / UP)
        gg = wsum[slot, h] * jnp.tanh(half) + wdif[slot, h]
        g1, g2 = split(gg)
        wide = dot(g1, ccat)
        gv[...] += wide[:, :width] + wide[:, width:] + dot(g2, chi)
        tall = dot(g1, vcat[...], TN)
        return tall[:, :width] + tall[:, width:] + dot(g2, vcat[:, :width], TN)

    def sweep(slot, ctx, first, count, into):
        @pl.loop(0, count, unroll=2)
        def _(j):
            into[pl.ds(pl.multiple_of(j * LANE, LANE), LANE), :] = chunk(slot, ctx, first + j)

    def take(v):
        vhi, vlo = split(v)
        vcat[...] = jnp.concatenate([vhi, vlo], axis=1)
        v8[...] = jnp.concatenate([small(vlo, UP), small(vhi, 1.0)], axis=1)
        gv[...] = jnp.zeros((rows, width), F32)

    def middle(t, ctx):
        sweep(t % 2, ctx, 2, chunks - 4, gm)

    def rims(t, side, ctx):
        sweep(t % 2, ctx, side * (chunks - 2), 2, gs.at[t, side])
        guard(side, lambda: rim(t, side).start())

    guard(1, lambda: halo(1).start())
    for k in range(4):
        edge(1, k).start()
    counts(0, lambda: guard(0, lambda: halo(0).start()))
    for k in range(4):
        edge(2, k).start()

    cext[STRIP : STRIP + rows] = c_in[...]
    take(v_in[...])
    enter(0)
    rims(0, 0, cext)
    middle(0, cext)
    enter(1)
    rims(0, 1, cext)
    vnew[0] = v_in[...] - LR * gv[...]
    hop(0).start()
    cext[zone:rows] -= LR * gm[...]
    counts(1)

    hop(0).wait_recv()
    take(vrecv[0])
    middle(1, cext)
    cext[zone:rows] -= LR * gm[...]
    cross(2).start()
    for side in (1, 0):
        settle(0, side, cext)
        rims(1, side, cext)
    stay = vrecv[0] - LR * gv[...]
    vrecv[0] = stay
    take(stay)
    counts(2)

    settle(1, 0, cext)
    cross(0).start()
    cross(2).wait_recv()
    middle(2, cnext)
    cnext[zone:rows] -= LR * gm[...]
    settle(1, 1, cext)
    cross(1).start()
    for side in (0, 1):
        cross(side).wait_recv()
        rims(2, side, cnext)
    vnew[1] = vrecv[0] - LR * gv[...]
    hop(2).start()
    counts(3)

    hop(2).wait_recv()
    take(vrecv[1])
    middle(3, cnext)
    clast[own(2)] = cnext[zone:rows] - LR * gm[...]
    home(2).start()
    for side in (1, 0):
        settle(2, side, cnext)
        rims(3, side, cnext)
    vout[...] = vrecv[1] - LR * gv[...]
    for side in (0, 1):
        finish(side)
    for side in (2, 0, 1):
        home(side).wait_recv()
        cout[own(side)] = cfin[own(side)]

    for side in range(2):
        guard(side, lambda: halo(side).wait_send())
    for t in range(strata):
        for side in range(2):
            guard(side, lambda: rim(t, side).wait_send())
    for t in (0, 2):
        hop(t).wait_send()
    for t in (1, 2):
        for k in range(4):
            edge(t, k).wait_send()
    for side in range(3):
        cross(side).wait_send()
        home(side).wait_send()


def hand_on(v, c, vout, cout):
    vout[...] = v[...]
    cout[...] = c[...]


def local(vertex, context, edge_source, edge_target, edge_weight, negative_rows):
    strata, _, blocks, slots = edge_source.shape
    negs = negative_rows.shape[3]
    rows, width = vertex.shape
    ext = rows + 2 * STRIP
    chunks = ext // LANE
    flat = (strata, blocks, slots)
    vm = pl.BlockSpec(memory_space=pltpu.VMEM)
    sem = pltpu.SemaphoreType.DMA
    i32 = jnp.int32
    final = pl.pallas_call(
        kernel,
        out_shape=(jax.ShapeDtypeStruct((rows, width), F32),) * 2,
        in_specs=[vm] * 6,
        out_specs=(vm, vm),
        scratch_shapes=[
            pltpu.VMEM((2, chunks, rows, LANE), F32),
            pltpu.VMEM((2, chunks, rows, LANE), F32),
            pltpu.VMEM((2, blocks, slots), i32),
            pltpu.VMEM((2, blocks, slots), i32),
            pltpu.VMEM((2, blocks, slots), i32),
            pltpu.VMEM((2, negs, blocks, slots), i32),
            pltpu.VMEM((2, rows, width), F32),
            pltpu.VMEM((2, rows, width), F32),
            pltpu.VMEM((strata, 2, 2 * STRIP, width), F32),
            pltpu.VMEM((strata, 2, 2 * STRIP, width), F32),
            pltpu.VMEM((rows - 2 * STRIP, width), F32),
            pltpu.VMEM((rows, width), F32),
            pltpu.VMEM((ext, width), F32),
            pltpu.VMEM((ext, width), F32),
            pltpu.VMEM((rows, width), F32),
            pltpu.VMEM((rows, width), F32),
            pltpu.VMEM((2, STRIP, width), F32),
            pltpu.VMEM((rows, 2 * width), BF),
            pltpu.VMEM((rows, 2 * width), F8),
            sem((8,)),
            sem((8,)),
            sem((2,)),
            sem((2,)),
            sem((strata, 2)),
            sem((strata, 2)),
            sem((2,)),
            sem((2,)),
            sem((2, 3)),
            sem((2, 3)),
        ],
        compiler_params=pltpu.CompilerParams(
            collective_id=0, has_side_effects=True, vmem_limit_bytes=60 * 1024 * 1024
        ),
    )(
        vertex,
        context,
        edge_source.reshape(flat),
        edge_target.reshape(flat),
        edge_weight.reshape(flat),
        negative_rows.reshape(strata, blocks, negs, slots).transpose(0, 2, 1, 3),
    )
    return pl.pallas_call(
        hand_on,
        out_shape=(jax.ShapeDtypeStruct((rows, width), F32),) * 2,
        in_specs=[vm] * 2,
        out_specs=(vm, vm),
    )(*final)


def solution(mesh):
    lead = P(("grp", "mem"), None)
    edges = P(None, "grp", "mem", None)
    return jax.shard_map(
        local,
        mesh=mesh,
        in_specs=(lead, lead, edges, edges, edges, P(None, "grp", "mem", None, None)),
        out_specs=(lead, lead),
        check_vma=False,
    )
```

```python
import functools

import jax
import jax.numpy as jnp
from jax import lax
from jax.experimental import pallas as pl
from jax.experimental.pallas import tpu as pltpu
from jax.sharding import PartitionSpec as P

LR = 0.05
STRIP = 256
LANE = 256
BF = jnp.bfloat16
F8 = jnp.float8_e4m3fn
F32 = jnp.float32
NT = (((1,), (1,)), ((), ()))
NN = (((1,), (0,)), ((), ()))
TN = (((0,), (0,)), ((), ()))
UP = 256.0
TOP = 448.0


def dot(a, b, dims=NN):
    return lax.dot_general(a, b, dims, preferred_element_type=F32)


def split(x):
    hi = x.astype(BF)
    return hi, (x - hi.astype(F32)).astype(BF)


def small(x, scale):
    return jnp.clip(x.astype(F32) * scale, -TOP, TOP).astype(F8)


def row_bf(x):
    return x.astype(F32).astype(BF)


def count_tile(b, src, tgt, w, neg, wsum, wdif, rowblk):
    slots = src.shape[1]
    chunks = wsum.shape[0]
    one = jnp.ones((), BF)
    zero = jnp.zeros((), BF)
    iota_r = row_bf(lax.broadcasted_iota(jnp.int32, (rowblk, slots), 0))
    iota_c = row_bf(lax.broadcasted_iota(jnp.int32, (LANE, slots), 0))
    s1 = jnp.where(iota_r == row_bf(src), row_bf(w) * jnp.asarray(0.5, BF), zero)

    def hot(x):
        return jnp.where(iota_c == row_bf(x & (LANE - 1)), one, zero).astype(F8)

    def tall(x, first, count):
        hi = (x >> 8) - first
        return jnp.concatenate(
            [(s1 * row_bf(jnp.where(hi == h, 1.0, 0.0))).astype(F8) for h in range(count)], axis=0
        )

    at = jnp.concatenate([tall(neg[n : n + 1], 0, chunks) for n in range(neg.shape[0])], axis=1)
    bt = jnp.concatenate([hot(neg[n : n + 1]) for n in range(neg.shape[0])], axis=1)
    cn = dot(at, bt, NT)
    first = b // 2
    cp = dot(tall(tgt, first, 3), hot(tgt), NT)
    rows = pl.ds(pl.multiple_of(b * rowblk, rowblk), rowblk)
    for h in range(chunks):
        wsum[h, rows, :] = cn[h * rowblk : (h + 1) * rowblk]
        wdif[h, rows, :] = cn[h * rowblk : (h + 1) * rowblk]
    for h in range(3):
        wsum[first + h, rows, :] += cp[h * rowblk : (h + 1) * rowblk]
        wdif[first + h, rows, :] -= cp[h * rowblk : (h + 1) * rowblk]


def flip(g, value):
    bit = 1
    while bit <= value:
        if value & bit:
            g = g + bit - 2 * bit * ((g // bit) % 2)
        bit *= 2
    return g


def gray(t):
    return t ^ (t >> 1)


def remote(src, dst, send, recv, **where):
    return pltpu.make_async_remote_copy(
        src_ref=src, dst_ref=dst, send_sem=send, recv_sem=recv,
        device_id=where, device_id_type=pl.DeviceIdType.MESH,
    )


def kernel(
    v_in, c_in, e_src, e_tgt, e_w, e_neg, vout, cout,
    wsum, wdif, r_src, r_tgt, r_w, r_neg, vnew, vrecv, gs, gr, gm, gv, cext, cnext, clast, cfin, chalo, vcat, v8,
    edge_send, edge_recv, halo_send, halo_recv, rim_send, rim_recv, v_send, v_recv, c_send, c_recv,
):
    strata, blocks, slots = e_src.shape
    rows, width = v_in.shape
    rowblk = rows // blocks
    chunks = wsum.shape[1]
    zone = 2 * STRIP
    g = lax.axis_index("grp")
    m = lax.axis_index("mem")
    members = lax.axis_size("mem")
    has_down = m > 0
    has_up = m < members - 1
    near, far = flip(g, 1), flip(g, 2)

    barrier = pltpu.get_barrier_semaphore()
    for partner in (near, far):
        pl.semaphore_signal(barrier, inc=1, device_id={"grp": partner}, device_id_type=pl.DeviceIdType.MESH)

    @pl.when(has_down)
    def _():
        pl.semaphore_signal(barrier, inc=1, device_id={"mem": m - 1}, device_id_type=pl.DeviceIdType.MESH)

    @pl.when(has_up)
    def _():
        pl.semaphore_signal(barrier, inc=1, device_id={"mem": m + 1}, device_id_type=pl.DeviceIdType.MESH)

    pl.semaphore_wait(barrier, 2 + jnp.where(has_down, 1, 0) + jnp.where(has_up, 1, 0))

    def halo(side):
        if side == 0:
            return remote(c_in.at[0:STRIP], chalo.at[1], halo_send.at[0], halo_recv.at[1], mem=m - 1)
        return remote(c_in.at[rows - STRIP : rows], chalo.at[0], halo_send.at[1], halo_recv.at[0], mem=m + 1)

    def rim(t, side):
        last = t == strata - 1
        if side == 0:
            span = slice(0, STRIP if last else zone)
            return remote(gs.at[t, 0, span], gr.at[t, 1, span], rim_send.at[t, 0], rim_recv.at[t, 1], mem=m - 1)
        span = slice(STRIP if last else 0, zone)
        return remote(gs.at[t, 1, span], gr.at[t, 0, span], rim_send.at[t, 1], rim_recv.at[t, 0], mem=m + 1)

    def hop(t):
        i = t // 2
        return remote(vnew.at[i], vrecv.at[i], v_send.at[i], v_recv.at[i], grp=near)

    def area(side):
        return slice(zone, rows) if side == 2 else slice(side * rows, side * rows + zone)

    def own(side):
        return (slice(0, STRIP), slice(rows - STRIP, rows), slice(STRIP, rows - STRIP))[side]

    def cross(side):
        span = area(side)
        return remote(cext.at[span], cnext.at[span], c_send.at[0, side], c_recv.at[0, side], grp=far)

    def home(side):
        span = own(side)
        return remote(clast.at[span], cfin.at[span], c_send.at[1, side], c_recv.at[1, side], grp=far)

    def edge(t, k):
        a = (e_src, e_tgt, e_w, e_neg)[k]
        z = (r_src, r_tgt, r_w, r_neg)[k]
        i = (t - 1) * 4 + k
        return remote(a.at[t], z.at[t - 1], edge_send.at[i], edge_recv.at[i], grp=near)

    def guard(side, action):
        @pl.when(has_down if side == 0 else has_up)
        def _():
            action()

    def counts(t, between=None, cut=4):
        if t in (0, strata - 1):
            a, b_, c, d = e_src.at[t], e_tgt.at[t], e_w.at[t], e_neg.at[t]
        else:
            for k in range(4):
                edge(t, k).wait_recv()
            a, b_, c, d = r_src.at[t - 1], r_tgt.at[t - 1], r_w.at[t - 1], r_neg.at[t - 1]

        def run(lo, hi):
            @pl.loop(lo, hi, unroll=2)
            def _(b):
                one = pl.ds(b, 1)
                count_tile(b, a[one, :], b_[one, :], c[one, :], jnp.concatenate([d[n, one, :] for n in range(d.shape[0])], axis=0), wsum.at[t % 2], wdif.at[t % 2], rowblk)

        if between is None:
            run(0, blocks)
        else:
            run(0, blocks * cut // 8)
            between()
            run(blocks * cut // 8, blocks)

    def enter(side):
        there = has_down if side == 0 else has_up
        span = slice(0, STRIP) if side == 0 else slice(STRIP + rows, rows + 2 * STRIP)

        @pl.when(there)
        def _():
            halo(1 - side).wait_recv()
            cext[span] = chalo[side]

        @pl.when(jnp.logical_not(there))
        def _():
            cext[span] = jnp.zeros((STRIP, width), F32)

    def settle(t, side, ctx):
        there = has_down if side == 0 else has_up
        base = side * rows
        mine = slice(base + STRIP, base + zone) if side == 0 else slice(base, base + STRIP)
        off = slice(STRIP, zone) if side == 0 else slice(0, STRIP)

        @pl.when(there)
        def _():
            rim(t, 1 - side).wait_recv()
            ctx[base : base + zone] -= LR * (gs[t, side] + gr[t, side])

        @pl.when(jnp.logical_not(there))
        def _():
            ctx[mine] -= LR * gs[t, side, off]

    def finish(side):
        t = strata - 1
        there = has_down if side == 0 else has_up
        base = side * rows
        mine = slice(base + STRIP, base + zone) if side == 0 else slice(base, base + STRIP)
        off = slice(STRIP, zone) if side == 0 else slice(0, STRIP)
        to = own(side)

        @pl.when(there)
        def _():
            rim(t, 1 - side).wait_recv()
            clast[to] = cnext[mine] - LR * (gs[t, side, off] + gr[t, side, off])

        @pl.when(jnp.logical_not(there))
        def _():
            clast[to] = cnext[mine] - LR * gs[t, side, off]

        home(side).start()

    def chunk(slot, ctx, h):
        c = ctx[pl.ds(pl.multiple_of(h * LANE, LANE), LANE), :]
        chi, clo = split(c)
        ccat = jnp.concatenate([chi, clo], axis=1)
        chalf = (chi.astype(F32) * 0.5).astype(BF)
        c8 = jnp.concatenate([small(chi, 0.5), small(clo, 0.5 * UP)], axis=1)
        half = dot(vcat[:, :width], chalf, NT) + dot(v8[...], c8, NT) * (1.0 / UP)
        gg = wsum[slot, h] * jnp.tanh(half) + wdif[slot, h]
        g1, g2 = split(gg)
        wide = dot(g1, ccat)
        gv[...] += wide[:, :width] + wide[:, width:] + dot(g2, chi)
        tall = dot(g1, vcat[...], TN)
        return tall[:, :width] + tall[:, width:] + dot(g2, vcat[:, :width], TN)

    def sweep(slot, ctx, first, count, into):
        @pl.loop(0, count, unroll=2)
        def _(j):
            into[pl.ds(pl.multiple_of(j * LANE, LANE), LANE), :] = chunk(slot, ctx, first + j)

    def take(v):
        vhi, vlo = split(v)
        vcat[...] = jnp.concatenate([vhi, vlo], axis=1)
        v8[...] = jnp.concatenate([small(vlo, UP), small(vhi, 1.0)], axis=1)
        gv[...] = jnp.zeros((rows, width), F32)

    def middle(t, ctx):
        sweep(t % 2, ctx, 2, chunks - 4, gm)

    def rims(t, side, ctx):
        sweep(t % 2, ctx, side * (chunks - 2), 2, gs.at[t, side])
        guard(side, lambda: rim(t, side).start())

    guard(1, lambda: halo(1).start())
    for k in range(4):
        edge(1, k).start()
    counts(0, lambda: guard(0, lambda: halo(0).start()))
    for k in range(4):
        edge(2, k).start()

    cext[STRIP : STRIP + rows] = c_in[...]
    take(v_in[...])
    enter(0)
    rims(0, 0, cext)
    middle(0, cext)
    enter(1)
    rims(0, 1, cext)
    vnew[0] = v_in[...] - LR * gv[...]
    hop(0).start()
    cext[zone:rows] -= LR * gm[...]
    counts(1)

    hop(0).wait_recv()
    take(vrecv[0])
    settle(0, 1, cext)
    rims(1, 1, cext)
    middle(1, cext)
    cext[zone:rows] -= LR * gm[...]
    cross(2).start()
    settle(0, 0, cext)
    rims(1, 0, cext)
    stay = vrecv[0] - LR * gv[...]
    vrecv[0] = stay
    take(stay)
    def pass_on():
        settle(1, 0, cext)
        cross(0).start()

    counts(2, pass_on)
    cross(2).wait_recv()
    settle(1, 1, cext)
    cross(1).start()
    middle(2, cnext)
    cnext[zone:rows] -= LR * gm[...]
    cross(0).wait_recv()
    rims(2, 0, cnext)

    def last_zone():
        cross(1).wait_recv()
        rims(2, 1, cnext)
        vnew[1] = vrecv[0] - LR * gv[...]
        hop(2).start()

    counts(3, last_zone, 2)

    hop(2).wait_recv()
    take(vrecv[1])
    middle(3, cnext)
    clast[own(2)] = cnext[zone:rows] - LR * gm[...]
    home(2).start()
    for side in (1, 0):
        settle(2, side, cnext)
        rims(3, side, cnext)
    vout[...] = vrecv[1] - LR * gv[...]
    for side in (0, 1):
        finish(side)
    for side in (2, 0, 1):
        home(side).wait_recv()
        cout[own(side)] = cfin[own(side)]

    for side in range(2):
        guard(side, lambda: halo(side).wait_send())
    for t in range(strata):
        for side in range(2):
            guard(side, lambda: rim(t, side).wait_send())
    for t in (0, 2):
        hop(t).wait_send()
    for t in (1, 2):
        for k in range(4):
            edge(t, k).wait_send()
    for side in range(3):
        cross(side).wait_send()
        home(side).wait_send()


def hand_on(v, c, vout, cout):
    vout[...] = v[...]
    cout[...] = c[...]


def local(vertex, context, edge_source, edge_target, edge_weight, negative_rows):
    strata, _, blocks, slots = edge_source.shape
    negs = negative_rows.shape[3]
    rows, width = vertex.shape
    ext = rows + 2 * STRIP
    chunks = ext // LANE
    flat = (strata, blocks, slots)
    vm = pl.BlockSpec(memory_space=pltpu.VMEM)
    sem = pltpu.SemaphoreType.DMA
    i32 = jnp.int32
    final = pl.pallas_call(
        kernel,
        out_shape=(jax.ShapeDtypeStruct((rows, width), F32),) * 2,
        in_specs=[vm] * 6,
        out_specs=(vm, vm),
        scratch_shapes=[
            pltpu.VMEM((2, chunks, rows, LANE), F32),
            pltpu.VMEM((2, chunks, rows, LANE), F32),
            pltpu.VMEM((2, blocks, slots), i32),
            pltpu.VMEM((2, blocks, slots), i32),
            pltpu.VMEM((2, blocks, slots), i32),
            pltpu.VMEM((2, negs, blocks, slots), i32),
            pltpu.VMEM((2, rows, width), F32),
            pltpu.VMEM((2, rows, width), F32),
            pltpu.VMEM((strata, 2, 2 * STRIP, width), F32),
            pltpu.VMEM((strata, 2, 2 * STRIP, width), F32),
            pltpu.VMEM((rows - 2 * STRIP, width), F32),
            pltpu.VMEM((rows, width), F32),
            pltpu.VMEM((ext, width), F32),
            pltpu.VMEM((ext, width), F32),
            pltpu.VMEM((rows, width), F32),
            pltpu.VMEM((rows, width), F32),
            pltpu.VMEM((2, STRIP, width), F32),
            pltpu.VMEM((rows, 2 * width), BF),
            pltpu.VMEM((rows, 2 * width), F8),
            sem((8,)),
            sem((8,)),
            sem((2,)),
            sem((2,)),
            sem((strata, 2)),
            sem((strata, 2)),
            sem((2,)),
            sem((2,)),
            sem((2, 3)),
            sem((2, 3)),
        ],
        compiler_params=pltpu.CompilerParams(
            collective_id=0, has_side_effects=True, vmem_limit_bytes=60 * 1024 * 1024
        ),
    )(
        vertex,
        context,
        edge_source.reshape(flat),
        edge_target.reshape(flat),
        edge_weight.reshape(flat),
        negative_rows.reshape(strata, blocks, negs, slots).transpose(0, 2, 1, 3),
    )
    return pl.pallas_call(
        hand_on,
        out_shape=(jax.ShapeDtypeStruct((rows, width), F32),) * 2,
        in_specs=[vm] * 2,
        out_specs=(vm, vm),
    )(*final)


def solution(mesh):
    lead = P(("grp", "mem"), None)
    edges = P(None, "grp", "mem", None)
    return jax.shard_map(
        local,
        mesh=mesh,
        in_specs=(lead, lead, edges, edges, edges, P(None, "grp", "mem", None, None)),
        out_specs=(lead, lead),
        check_vma=False,
    )
```

```python
import functools

import jax
import jax.numpy as jnp
from jax import lax
from jax.experimental import pallas as pl
from jax.experimental.pallas import tpu as pltpu
from jax.sharding import PartitionSpec as P

LR = 0.05
STRIP = 256
LANE = 256
BF = jnp.bfloat16
F8 = jnp.float8_e4m3fn
F32 = jnp.float32
NT = (((1,), (1,)), ((), ()))
NN = (((1,), (0,)), ((), ()))
TN = (((0,), (0,)), ((), ()))
UP = 256.0
TOP = 448.0


def dot(a, b, dims=NN):
    return lax.dot_general(a, b, dims, preferred_element_type=F32)


def split(x):
    hi = x.astype(BF)
    return hi, (x - hi.astype(F32)).astype(BF)


def small(x, scale):
    return jnp.clip(x.astype(F32) * scale, -TOP, TOP).astype(F8)


def row_bf(x):
    return x.astype(F32).astype(BF)


def count_tile(b, src, tgt, w, neg, wsum, wdif, rowblk):
    slots = src.shape[1]
    chunks = wsum.shape[0]
    one = jnp.ones((), BF)
    zero = jnp.zeros((), BF)
    iota_r = row_bf(lax.broadcasted_iota(jnp.int32, (rowblk, slots), 0))
    iota_c = row_bf(lax.broadcasted_iota(jnp.int32, (LANE, slots), 0))
    s1 = jnp.where(iota_r == row_bf(src), row_bf(w) * jnp.asarray(0.5, BF), zero)

    def hot(x):
        return jnp.where(iota_c == row_bf(x & (LANE - 1)), one, zero).astype(F8)

    def tall(x, first, count):
        hi = (x >> 8) - first
        return jnp.concatenate(
            [(s1 * row_bf(jnp.where(hi == h, 1.0, 0.0))).astype(F8) for h in range(count)], axis=0
        )

    at = jnp.concatenate([tall(neg[n : n + 1], 0, chunks) for n in range(neg.shape[0])], axis=1)
    bt = jnp.concatenate([hot(neg[n : n + 1]) for n in range(neg.shape[0])], axis=1)
    cn = dot(at, bt, NT)
    first = b // 2
    cp = dot(tall(tgt, first, 3), hot(tgt), NT)
    rows = pl.ds(pl.multiple_of(b * rowblk, rowblk), rowblk)
    for h in range(chunks):
        wsum[h, rows, :] = cn[h * rowblk : (h + 1) * rowblk]
        wdif[h, rows, :] = cn[h * rowblk : (h + 1) * rowblk]
    for h in range(3):
        wsum[first + h, rows, :] += cp[h * rowblk : (h + 1) * rowblk]
        wdif[first + h, rows, :] -= cp[h * rowblk : (h + 1) * rowblk]


def flip(g, value):
    bit = 1
    while bit <= value:
        if value & bit:
            g = g + bit - 2 * bit * ((g // bit) % 2)
        bit *= 2
    return g


def gray(t):
    return t ^ (t >> 1)


def remote(src, dst, send, recv, **where):
    return pltpu.make_async_remote_copy(
        src_ref=src, dst_ref=dst, send_sem=send, recv_sem=recv,
        device_id=where, device_id_type=pl.DeviceIdType.MESH,
    )


def kernel(
    v_in, c_in, e_src, e_tgt, e_w, e_neg, vout, cout,
    wsum, wdif, r_src, r_tgt, r_w, r_neg, vnew, vrecv, gs, gr, gm, gv, cext, cnext, clast, cfin, chalo, vcat, v8,
    edge_send, edge_recv, halo_send, halo_recv, rim_send, rim_recv, v_send, v_recv, c_send, c_recv,
):
    strata, blocks, slots = e_src.shape
    rows, width = v_in.shape
    rowblk = rows // blocks
    chunks = wsum.shape[1]
    zone = 2 * STRIP
    g = lax.axis_index("grp")
    m = lax.axis_index("mem")
    members = lax.axis_size("mem")
    has_down = m > 0
    has_up = m < members - 1
    near, far = flip(g, 1), flip(g, 2)

    barrier = pltpu.get_barrier_semaphore()
    for partner in (near, far):
        pl.semaphore_signal(barrier, inc=1, device_id={"grp": partner}, device_id_type=pl.DeviceIdType.MESH)

    @pl.when(has_down)
    def _():
        pl.semaphore_signal(barrier, inc=1, device_id={"mem": m - 1}, device_id_type=pl.DeviceIdType.MESH)

    @pl.when(has_up)
    def _():
        pl.semaphore_signal(barrier, inc=1, device_id={"mem": m + 1}, device_id_type=pl.DeviceIdType.MESH)

    pl.semaphore_wait(barrier, 2 + jnp.where(has_down, 1, 0) + jnp.where(has_up, 1, 0))

    def halo(side):
        if side == 0:
            return remote(c_in.at[0:STRIP], chalo.at[1], halo_send.at[0], halo_recv.at[1], mem=m - 1)
        return remote(c_in.at[rows - STRIP : rows], chalo.at[0], halo_send.at[1], halo_recv.at[0], mem=m + 1)

    def rim(t, side):
        last = t == strata - 1
        if side == 0:
            span = slice(0, STRIP if last else zone)
            return remote(gs.at[t, 0, span], gr.at[t, 1, span], rim_send.at[t, 0], rim_recv.at[t, 1], mem=m - 1)
        span = slice(STRIP if last else 0, zone)
        return remote(gs.at[t, 1, span], gr.at[t, 0, span], rim_send.at[t, 1], rim_recv.at[t, 0], mem=m + 1)

    def hop(t):
        i = t // 2
        return remote(vnew.at[i], vrecv.at[i], v_send.at[i], v_recv.at[i], grp=near)

    def area(side):
        return slice(zone, rows) if side == 2 else slice(side * rows, side * rows + zone)

    def own(side):
        return (slice(0, STRIP), slice(rows - STRIP, rows), slice(STRIP, rows - STRIP))[side]

    def cross(side):
        span = area(side)
        return remote(cext.at[span], cnext.at[span], c_send.at[0, side], c_recv.at[0, side], grp=far)

    def home(side):
        span = own(side)
        return remote(clast.at[span], cfin.at[span], c_send.at[1, side], c_recv.at[1, side], grp=far)

    def edge(t, k):
        a = (e_src, e_tgt, e_w, e_neg)[k]
        z = (r_src, r_tgt, r_w, r_neg)[k]
        i = (t - 1) * 4 + k
        return remote(a.at[t], z.at[t - 1], edge_send.at[i], edge_recv.at[i], grp=near)

    def guard(side, action):
        @pl.when(has_down if side == 0 else has_up)
        def _():
            action()

    def counts(t, between=None, cut=4):
        if t in (0, strata - 1):
            a, b_, c, d = e_src.at[t], e_tgt.at[t], e_w.at[t], e_neg.at[t]
        else:
            for k in range(4):
                edge(t, k).wait_recv()
            a, b_, c, d = r_src.at[t - 1], r_tgt.at[t - 1], r_w.at[t - 1], r_neg.at[t - 1]

        def run(lo, hi):
            @pl.loop(lo, hi, unroll=2)
            def _(b):
                one = pl.ds(b, 1)
                count_tile(b, a[one, :], b_[one, :], c[one, :], jnp.concatenate([d[n, one, :] for n in range(d.shape[0])], axis=0), wsum.at[t % 2], wdif.at[t % 2], rowblk)

        if between is None:
            run(0, blocks)
        else:
            run(0, blocks * cut // 8)
            between()
            run(blocks * cut // 8, blocks)

    def enter(side):
        there = has_down if side == 0 else has_up
        span = slice(0, STRIP) if side == 0 else slice(STRIP + rows, rows + 2 * STRIP)

        @pl.when(there)
        def _():
            halo(1 - side).wait_recv()
            cext[span] = chalo[side]

        @pl.when(jnp.logical_not(there))
        def _():
            cext[span] = jnp.zeros((STRIP, width), F32)

    def settle(t, side, ctx):
        there = has_down if side == 0 else has_up
        base = side * rows
        mine = slice(base + STRIP, base + zone) if side == 0 else slice(base, base + STRIP)
        off = slice(STRIP, zone) if side == 0 else slice(0, STRIP)

        @pl.when(there)
        def _():
            rim(t, 1 - side).wait_recv()
            ctx[base : base + zone] -= LR * (gs[t, side] + gr[t, side])

        @pl.when(jnp.logical_not(there))
        def _():
            ctx[mine] -= LR * gs[t, side, off]

    def finish(side):
        t = strata - 1
        there = has_down if side == 0 else has_up
        base = side * rows
        mine = slice(base + STRIP, base + zone) if side == 0 else slice(base, base + STRIP)
        off = slice(STRIP, zone) if side == 0 else slice(0, STRIP)
        to = own(side)

        @pl.when(there)
        def _():
            rim(t, 1 - side).wait_recv()
            clast[to] = cnext[mine] - LR * (gs[t, side, off] + gr[t, side, off])

        @pl.when(jnp.logical_not(there))
        def _():
            clast[to] = cnext[mine] - LR * gs[t, side, off]

        home(side).start()

    def chunk(slot, ctx, h):
        c = ctx[pl.ds(pl.multiple_of(h * LANE, LANE), LANE), :]
        chi, clo = split(c)
        ccat = jnp.concatenate([chi, clo], axis=1)
        chalf = (chi.astype(F32) * 0.5).astype(BF)
        c8 = jnp.concatenate([small(chi, 0.5), small(clo, 0.5 * UP)], axis=1)
        half = dot(vcat[:, :width], chalf, NT) + dot(v8[...], c8, NT) * (1.0 / UP)
        gg = wsum[slot, h] * jnp.tanh(half) + wdif[slot, h]
        g1, g2 = split(gg)
        wide = dot(g1, ccat)
        gv[...] += wide[:, :width] + wide[:, width:] + dot(g2, chi)
        tall = dot(g1, vcat[...], TN)
        return tall[:, :width] + tall[:, width:] + dot(g2, vcat[:, :width], TN)

    def sweep(slot, ctx, first, count, into):
        @pl.loop(0, count, unroll=2)
        def _(j):
            into[pl.ds(pl.multiple_of(j * LANE, LANE), LANE), :] = chunk(slot, ctx, first + j)

    def take(v):
        vhi, vlo = split(v)
        vcat[...] = jnp.concatenate([vhi, vlo], axis=1)
        v8[...] = jnp.concatenate([small(vlo, UP), small(vhi, 1.0)], axis=1)
        gv[...] = jnp.zeros((rows, width), F32)

    def middle(t, ctx):
        sweep(t % 2, ctx, 2, chunks - 4, gm)

    def rims(t, side, ctx):
        sweep(t % 2, ctx, side * (chunks - 2), 2, gs.at[t, side])
        guard(side, lambda: rim(t, side).start())

    guard(1, lambda: halo(1).start())
    for k in range(4):
        edge(1, k).start()
    counts(0, lambda: guard(0, lambda: halo(0).start()))
    for k in range(4):
        edge(2, k).start()

    cext[STRIP : STRIP + rows] = c_in[...]
    take(v_in[...])
    enter(0)
    rims(0, 0, cext)
    middle(0, cext)
    enter(1)
    rims(0, 1, cext)
    vnew[0] = v_in[...] - LR * gv[...]
    hop(0).start()
    cext[zone:rows] -= LR * gm[...]
    counts(1)

    hop(0).wait_recv()
    take(vrecv[0])
    settle(0, 1, cext)
    rims(1, 1, cext)
    middle(1, cext)
    cext[zone:rows] -= LR * gm[...]
    cross(2).start()
    settle(0, 0, cext)
    rims(1, 0, cext)
    stay = vrecv[0] - LR * gv[...]
    vrecv[0] = stay
    take(stay)
    def pass_on():
        settle(1, 0, cext)
        cross(0).start()

    counts(2, pass_on, 2)
    cross(2).wait_recv()
    settle(1, 1, cext)
    cross(1).start()
    middle(2, cnext)
    cnext[zone:rows] -= LR * gm[...]
    cross(0).wait_recv()
    rims(2, 0, cnext)

    def last_zone():
        cross(1).wait_recv()
        rims(2, 1, cnext)
        vnew[1] = vrecv[0] - LR * gv[...]
        hop(2).start()

    counts(3, last_zone, 2)

    hop(2).wait_recv()
    take(vrecv[1])
    middle(3, cnext)
    clast[own(2)] = cnext[zone:rows] - LR * gm[...]
    home(2).start()
    for side in (1, 0):
        settle(2, side, cnext)
        rims(3, side, cnext)
    vout[...] = vrecv[1] - LR * gv[...]
    for side in (0, 1):
        finish(side)
    for side in (2, 0, 1):
        home(side).wait_recv()
        cout[own(side)] = cfin[own(side)]

    for side in range(2):
        guard(side, lambda: halo(side).wait_send())
    for t in range(strata):
        for side in range(2):
            guard(side, lambda: rim(t, side).wait_send())
    for t in (0, 2):
        hop(t).wait_send()
    for t in (1, 2):
        for k in range(4):
            edge(t, k).wait_send()
    for side in range(3):
        cross(side).wait_send()
        home(side).wait_send()


def hand_on(v, c, vout, cout):
    vout[...] = v[...]
    cout[...] = c[...]


def local(vertex, context, edge_source, edge_target, edge_weight, negative_rows):
    strata, _, blocks, slots = edge_source.shape
    negs = negative_rows.shape[3]
    rows, width = vertex.shape
    ext = rows + 2 * STRIP
    chunks = ext // LANE
    flat = (strata, blocks, slots)
    vm = pl.BlockSpec(memory_space=pltpu.VMEM)
    sem = pltpu.SemaphoreType.DMA
    i32 = jnp.int32
    final = pl.pallas_call(
        kernel,
        out_shape=(jax.ShapeDtypeStruct((rows, width), F32),) * 2,
        in_specs=[vm] * 6,
        out_specs=(vm, vm),
        scratch_shapes=[
            pltpu.VMEM((2, chunks, rows, LANE), F32),
            pltpu.VMEM((2, chunks, rows, LANE), F32),
            pltpu.VMEM((2, blocks, slots), i32),
            pltpu.VMEM((2, blocks, slots), i32),
            pltpu.VMEM((2, blocks, slots), i32),
            pltpu.VMEM((2, negs, blocks, slots), i32),
            pltpu.VMEM((2, rows, width), F32),
            pltpu.VMEM((2, rows, width), F32),
            pltpu.VMEM((strata, 2, 2 * STRIP, width), F32),
            pltpu.VMEM((strata, 2, 2 * STRIP, width), F32),
            pltpu.VMEM((rows - 2 * STRIP, width), F32),
            pltpu.VMEM((rows, width), F32),
            pltpu.VMEM((ext, width), F32),
            pltpu.VMEM((ext, width), F32),
            pltpu.VMEM((rows, width), F32),
            pltpu.VMEM((rows, width), F32),
            pltpu.VMEM((2, STRIP, width), F32),
            pltpu.VMEM((rows, 2 * width), BF),
            pltpu.VMEM((rows, 2 * width), F8),
            sem((8,)),
            sem((8,)),
            sem((2,)),
            sem((2,)),
            sem((strata, 2)),
            sem((strata, 2)),
            sem((2,)),
            sem((2,)),
            sem((2, 3)),
            sem((2, 3)),
        ],
        compiler_params=pltpu.CompilerParams(
            collective_id=0, has_side_effects=True, vmem_limit_bytes=60 * 1024 * 1024
        ),
    )(
        vertex,
        context,
        edge_source.reshape(flat),
        edge_target.reshape(flat),
        edge_weight.reshape(flat),
        negative_rows.reshape(strata, blocks, negs, slots).transpose(0, 2, 1, 3),
    )
    return pl.pallas_call(
        hand_on,
        out_shape=(jax.ShapeDtypeStruct((rows, width), F32),) * 2,
        in_specs=[vm] * 2,
        out_specs=(vm, vm),
    )(*final)


def solution(mesh):
    lead = P(("grp", "mem"), None)
    edges = P(None, "grp", "mem", None)
    return jax.shard_map(
        local,
        mesh=mesh,
        in_specs=(lead, lead, edges, edges, edges, P(None, "grp", "mem", None, None)),
        out_specs=(lead, lead),
        check_vma=False,
    )
```
